256 devices in a mesh: slab: 32 (over y, x, z_lo), blk: 8 (over z_hi, core).
Axes of the slice: x: 4, y: 4, z: 8 (z_hi: 4, z_lo: 2; z = z_hi * 2 + z_lo), core: 2. Of those that a mesh axis runs over, the one named last changes fastest.
Arguments:
- interior: float32 [64, 512, 512], P('slab', 'blk'), may hold values from -6 to 6
- sources: float32 [64, 512, 512], P('slab', 'blk'), may hold values from -12 to 12
- absorption: float32 [64, 512, 512], P('slab', 'blk'), may hold values from 0.1 to 4
- bem_panel: bfloat16 [8192, 131072], P('blk', 'slab'), may hold values from -0.03125 to 0.03125
- incident: bfloat16 [131072, 512], P('slab'), may hold values from -160 to 160
- node_cell: int32 [131072], P('slab'), may hold values from 0 to 255
- offset: int32 [1], replicated, may hold values from 0 to 122880, as said below
Outputs:
- relaxed: float32 [64, 512, 512], P('slab', 'blk')
- boundary_flux: float32 [8192, 512], P(('blk', 'slab'))
The draws below stay inside these ranges and needn't reach their ends.
Inputs may be any that keep to these rules, and one draw needn't show every extreme that they name: offset is a multiple of 8192; rows offset to offset + 8191 lie among the 131072 boundary nodes.
All inputs are finite; a program needn't handle non-finite values.
Results may differ from the reference program's by a relative error of at most 0.0034.
Values sent between devices are 32-bit elements; how exact they have to be, the bound alone decides.
A program may use at most 64 MiB of HBM per device.

```python
import math
import jax
import jax.numpy as jnp
from jax import lax

CZ = 2
CY = 64
NX = 512
C_DEV = 512
PR = 8192
NRHS = 512
SWEEPS = 2
NZ = 64
NY = 512
NB = 131072
N_BLK = 8


def draw_incident(key, part):
    key_base, key_row, key_col = jax.random.split(key, 3)
    position = jnp.arange(NB, dtype=jnp.float32) / NB
    row_scale = 10.0 ** jax.random.uniform(key_row, (NB,), jnp.float32)
    col_scale = 10.0 ** jax.random.uniform(key_col, (NRHS,), jnp.float32)
    ramp = jnp.exp(jnp.log(3.0) * position)
    base = jnp.clip(jax.random.normal(key_base, (NB, NRHS), jnp.float32), -4.0, 4.0)
    values = 0.04 * base * (row_scale * ramp)[:, None] * col_scale[None, :]
    return values.astype(jnp.bfloat16)


def draw_offset(key, part):
    return (jax.random.randint(key, (1,), 0, NB // PR) * PR).astype(jnp.int32)


def touch_ends(result, key, smallest, largest):
    spot = [jax.random.randint(jax.random.fold_in(key, axis), (), 0, length) for axis, length in enumerate(result.shape)]
    main_axis = result.shape.index(max(result.shape))
    neighbour = spot[:main_axis] + [(spot[main_axis] + 1) % result.shape[main_axis]] + spot[main_axis + 1:]
    return result.at[tuple(spot)].set(smallest).at[tuple(neighbour)].set(largest)


def raised(values, key, source, target, blocks, factor):
    owner, partner = [(jnp.arange(values.shape[dim]) // (values.shape[dim] // blocks)).reshape([-1 if axis == dim else 1 for axis in range(values.ndim)]) for dim in (source, target)]
    chosen = jax.random.permutation(key, blocks)[partner]
    strong = (owner == chosen) | (owner == (partner + blocks // 2) % blocks)
    return jnp.where(strong, factor * values, values)


def block_scale(key, shape, pieces, least, largest):
    loudness, own = 1.0, jax.random.fold_in(key, 6)
    for dim, parts in pieces:
        heights = jnp.exp(jax.random.uniform(jax.random.fold_in(own, dim), (parts,), jnp.float32, least / len(pieces), largest / len(pieces)))
        loudness = loudness * jnp.repeat(heights, shape[dim] // parts).reshape([-1 if axis == dim else 1 for axis in range(len(shape))])
    return loudness


def gaussian(rng, shape, width, reach, cuts=(), held_as=jnp.bfloat16):
    entries = width * jax.random.normal(rng, shape, jnp.float32)
    if cuts:
        entries = entries * block_scale(rng, shape, cuts, -0.22, 0.18)
    return jnp.clip(entries, -reach, reach).astype(held_as)


def heavy_noise(key, shape, deviation, reach, cuts, heavy, kind=jnp.bfloat16):
    entries = deviation * jax.random.normal(key, shape, jnp.float32)
    if cuts:
        entries = entries * block_scale(key, shape, cuts, -0.22, 0.18)
    return jnp.clip(raised(entries, jax.random.fold_in(key, 3), *heavy), -reach, reach).astype(kind)


def setup_inputs(seed: int = 0) -> dict:
    key_list = jax.random.split(jax.random.key(seed), 8)
    return {
        "interior": gaussian(key_list[0], (NZ, NY, NX), 1.0, 6.0, ((0, 32), (1, 8)), jnp.float32),
        "sources": gaussian(key_list[1], (NZ, NY, NX), 2.0, 12.0, ((0, 32), (1, 8)), jnp.float32),
        "absorption": jnp.clip(jnp.exp(math.log(4.0) - 3.6888794 * jax.random.uniform(key_list[2], (NZ, NY, NX), jnp.float32) ** block_scale(key_list[2], (NZ, NY, NX), ((0, 32), (1, 8)), -0.2, 0.2)), 0.1, 4.0),
        "bem_panel": heavy_noise(key_list[3], (PR, NB), NB ** -0.5, 0.03125, ((0, 8), (1, 32)), (1, 0, 32, 2.75)),
        "incident": draw_incident(jax.random.fold_in(key_list[7], 71), 0),
        "node_cell": touch_ends(jax.random.randint(key_list[5], (NB,), 0, 2 * CZ * CY), jax.random.fold_in(key_list[5], 1), 0, (2 * CZ * CY) - 1).astype(jnp.int32),
        "offset": draw_offset(jax.random.fold_in(key_list[7], 71), 0),
    }


omega = 0.6
center_weight = 8.0 / 3.0

def stiffness(padded):
    along_x = padded[:, :, :-2] + padded[:, :, 2:]
    middle = padded[:, :, 1:-1]
    plus_mid = along_x + middle
    plane_sum = plus_mid[:, :-2] + plus_mid[:, 1:-1] + plus_mid[:, 2:]
    total_sum = plane_sum[:-2] + plane_sum[1:-1] + plane_sum[2:]
    cross_xy = along_x[:, :-2] + along_x[:, 2:]
    corner_sum = cross_xy[:-2] + cross_xy[2:]
    face_sum = along_x[1:-1, 1:-1] + middle[1:-1, :-2] + middle[1:-1, 2:] + middle[:-2, 1:-1] + middle[2:, 1:-1]
    center = middle[1:-1, 1:-1]
    edge_sum = total_sum - center - face_sum - corner_sum
    return center_weight * center - edge_sum / 6.0 - corner_sum / 12.0

def sweep_once(padded, sources, absorption):
    center = padded[1:-1, 1:-1, 1:-1]
    applied = stiffness(padded) + absorption * center
    return center + omega * (sources - applied) / (center_weight + absorption)

def reference(interior, sources, absorption, bem_panel, incident, node_cell, offset):
    current = interior
    for sweep_idx in range(SWEEPS):
        current = sweep_once(jnp.pad(current, 1), sources, absorption)
    nodes = jnp.arange(NB, dtype=jnp.int32)
    block = nodes // C_DEV
    zpos = block // N_BLK * CZ + node_cell // (2 * CY)
    ypos = block % N_BLK * CY + node_cell // 2 % CY
    xpos = node_cell % 2 * (NX - 1)
    trace = interior[zpos, ypos, xpos]
    fields = (incident.astype(jnp.float32) + trace[:, None]).astype(jnp.bfloat16)
    wide = fields.astype(jnp.float32)
    norms = jnp.sqrt(lax.optimization_barrier(jnp.sum(wide * wide, axis=0)) / NB + 1e-06)
    jump = lax.dynamic_slice_in_dim(wide, offset[0].astype(jnp.int32), PR, 0)
    product = jnp.dot(bem_panel, fields, preferred_element_type=jnp.float32) + 0.5 * jump
    return (current, product / norms[None, :])
```

```python
import jax
import jax.numpy as jnp
from jax import lax
from jax.experimental import pallas as pl
from jax.experimental.pallas import tpu as pltpu
from jax.sharding import PartitionSpec as P

F32 = jnp.float32
BF16 = jnp.bfloat16
MESH = pl.DeviceIdType.MESH
CENTER = 8.0 / 3.0


def flip(pos, low, high):
    if low:
        pos = pos + 1 - 2 * lax.rem(pos, 2)
    if high:
        pos = 3 - pos
    return pos


XA, XB, YA, YB = ("x", 1, 0), ("x", 0, 1), ("y", 1, 0), ("y", 0, 1)
ORDERS = ((XA, YA, XB, YB), (YA, XA, YB, XB), (XB, YB, XA, YA), (YB, XB, YA, XA))
NODES = 131072.0


def along_x(w, first, last):
    n = w.shape[1]
    left = jnp.where(first, 0.0, pltpu.roll(w, 1, 1))
    right = jnp.where(last, 0.0, pltpu.roll(w, n - 1, 1))
    return left + right


def kernel(
    offset, interior, sources, absorption, bem, incident, cells,
    relaxed, flux,
    pad1, pad2, src, inv, ytx1, ytx2, yrx1, yrx2,
    cell_v, ttx, trx, inc_v, fld, panel,
    prod, rx1, rx2, rx3, rx4, rx5, ntx, nrx,
    load_sem, inc_sem, panel_sem, halo_send, halo_recv,
    trace_send, trace_recv, rs_send, rs_recv, n_send, n_recv,
):
    slab, blk = lax.axis_index("slab"), lax.axis_index("blk")
    my_y, my_x, my_z = slab // 8, lax.rem(slab // 2, 4), lax.rem(slab, 2)

    def at(y, x, z):
        return y * 8 + x * 2 + z

    def toward(dim):
        if dim == "z":
            return (at(my_y, my_x, 1 - my_z), blk)
        axis, low, high = dim
        if axis == "x":
            return (at(my_y, flip(my_x, low, high), my_z), blk)
        return (at(flip(my_y, low, high), my_x, my_z), blk)

    up, down = lax.rem(slab + 1, 32), lax.rem(slab + 31, 32)
    east, west = lax.rem(blk + 1, 8), lax.rem(blk + 7, 8)

    core = pl.ds(8, 64)
    load_u = pltpu.make_async_copy(interior, pad1.at[pl.ds(1, 2), core], load_sem.at[0])
    load_c = pltpu.make_async_copy(cells, cell_v, load_sem.at[1])
    load_s = pltpu.make_async_copy(sources, src, load_sem.at[2])
    load_a = pltpu.make_async_copy(absorption, inv, load_sem.at[3])
    load_u.start()
    load_c.start()
    inc_loads = []
    for part in range(4):
        rows = pl.ds(part * 1024, 1024)
        inc_loads.append(pltpu.make_async_copy(incident.at[rows], inc_v.at[rows], inc_sem.at[part]))
        inc_loads[-1].start()

    partners = [(slab, lax.rem(blk + k, 8)) for k in range(1, 8)]
    partners += [toward(d) for d in (XA, XB, YA, YB, "z")]
    partners += [(up, blk), (down, blk), (up, east), (up, west), (down, east), (down, west)]
    barrier = pltpu.get_barrier_semaphore()
    for partner in partners:
        pl.semaphore_signal(barrier, inc=1, device_id=partner, device_id_type=MESH)

    panel_loads = []
    for q in (3, 2, 1, 0):
        for r in (3, 2, 1, 0):
            y = flip(my_y, q % 2, r % 2)
            x = flip(my_x, q // 2, r // 2)
            rows = pl.ds(pl.multiple_of(y * 256 + x * 64, 64), 64)
            panel_loads.append(pltpu.make_async_copy(bem.at[rows], panel.at[q, r], panel_sem.at[q, r]))
            panel_loads[-1].start()
    load_s.start()
    load_a.start()

    load_u.wait()
    load_c.wait()
    for z in range(2):
        for c in range(4):
            lanes = pl.ds(c * 128, 128)
            ytx1[0, pl.ds(z * 4 + c, 1), :] = pad1[1 + z, pl.ds(8, 1), lanes]
            ytx1[1, pl.ds(z * 4 + c, 1), :] = pad1[1 + z, pl.ds(71, 1), lanes]
    y_index = lax.broadcasted_iota(jnp.int32, (64, 128), 0) * 2
    for c in range(4):
        cell = cell_v[pl.ds(blk * 4 + c, 1), :]
        total = jnp.zeros((64, 128), F32)
        for z in range(2):
            for side in range(2):
                face = pad1[1 + z, pl.ds(8, 64), pl.ds(511 * side, 1)]
                total += jnp.where(cell == y_index + (z * 128 + side), face, 0.0)
        ttx[pl.ds(c, 1), :] = jnp.sum(total, axis=0, keepdims=True)
    ttx[pl.ds(4, 4), :] = jnp.zeros((4, 128), F32)
    trx[0] = ttx[...]

    pl.semaphore_wait(barrier, len(partners))

    traces = []
    for k in range(1, 8):
        traces.append(pltpu.make_async_remote_copy(
            src_ref=ttx, dst_ref=trx.at[k], send_sem=trace_send.at[k], recv_sem=trace_recv.at[k],
            device_id=(slab, lax.rem(blk + k, 8)), device_id_type=MESH))
        traces[-1].start()

    def halo_copies(sweep, pad, ytx, yrx):
        def copy(n, source, target, device):
            return pltpu.make_async_remote_copy(
                src_ref=source, dst_ref=target, send_sem=halo_send.at[sweep, n],
                recv_sem=halo_recv.at[sweep, n], device_id=device, device_id_type=MESH)
        return [
            copy(0, pad.at[2, core], pad.at[0, core], (up, blk)),
            copy(1, pad.at[1, core], pad.at[3, core], (down, blk)),
            copy(2, ytx.at[1], yrx.at[0], (slab, east)),
            copy(3, ytx.at[1], yrx.at[1], (up, east)),
            copy(4, ytx.at[1], yrx.at[2], (down, east)),
            copy(5, ytx.at[0], yrx.at[3], (slab, west)),
            copy(6, ytx.at[0], yrx.at[4], (up, west)),
            copy(7, ytx.at[0], yrx.at[5], (down, west)),
        ]

    halos1 = halo_copies(0, pad1, ytx1, yrx1)
    halos2 = halo_copies(1, pad2, ytx2, yrx2)
    for copy in halos1:
        copy.start()

    for copy in traces:
        copy.wait_recv()
    turned = jnp.concatenate([trx[...].reshape(64, 128), jnp.zeros((64, 128), F32)], axis=0).T
    for copy in inc_loads:
        copy.wait()
    for k in range(8):
        base = lax.rem(blk + 8 - k, 8) * 512
        for c in range(4):
            rows = pl.ds(pl.multiple_of(base + c * 128, 128), 128)
            column = lax.slice(turned, (0, k * 8 + c), (128, k * 8 + c + 1))
            fld[rows, :] = (inc_v[rows, :].astype(F32) + column).astype(BF16)

    wanted = offset[0] // 4096 + blk // 4
    hit = jnp.full((8, 128), wanted, jnp.int32) == jnp.full((8, 128), slab, jnp.int32)
    coef = jnp.where(hit, 0.5, 0.0).astype(F32)[0:1, 0:1]
    jump_base = lax.rem(blk, 4) * 1024

    boxes = (rx1, rx2, rx3, rx4)

    def rs_copy(part, stage, chunk):
        size = 512 >> stage
        half = size // 2
        start = 0 if chunk == 1 else half
        return pltpu.make_async_remote_copy(
            src_ref=prod.at[part, pl.ds(size + start, half)],
            dst_ref=boxes[stage].at[part, pl.ds(start, half)],
            send_sem=rs_send.at[part, stage, chunk], recv_sem=rs_recv.at[part, stage, chunk],
            device_id=toward(ORDERS[part][stage]), device_id_type=MESH)

    copies = {(p, s, c): rs_copy(p, s, c) for p in range(4) for s in range(4) for c in range(2)}

    for n, copy in enumerate(panel_loads):
        copy.wait()

    def swapped(q):
        return (q % 2) * 2 + q // 2

    def unit(pair, q):
        lhs = panel[q] if pair == 0 else panel[:, q]
        cols = pl.ds(pair * 256, 256)
        out = jnp.dot(lhs.reshape(256, 4096), fld[:, cols], preferred_element_type=F32)
        for r in range(4):
            qa, qb = (q, r) if pair == 0 else (r, q)
            y = flip(my_y, qa % 2, qb % 2)
            x = flip(my_x, qa // 2, qb // 2)
            rows = pl.ds(pl.multiple_of(jump_base + y * 256 + x * 64, 64), 64)
            piece = out[r * 64:(r + 1) * 64] + coef * fld[rows, cols].astype(F32)
            prod[pair * 2, pl.ds(q * 256 + r * 64, 64), :] = piece[:, :128]
            prod[pair * 2 + 1, pl.ds(swapped(q) * 256 + swapped(r) * 64, 64), :] = piece[:, 128:]

    for pair in range(2):
        unit(pair, 3)
        copies[pair * 2, 0, 0].start()
        copies[pair * 2 + 1, 0, 0].start()
    for pair in range(2):
        unit(pair, 2)
        copies[pair * 2, 0, 1].start()
    for pair in range(2):
        unit(pair, 1)
        copies[pair * 2 + 1, 0, 1].start()
    for pair in range(2):
        unit(pair, 0)

    def add_squares(n, total):
        x = fld[pl.ds(pl.multiple_of(n * 128, 128), 128), :].astype(F32)
        return total + jnp.sum((x * x).reshape(16, 8, 512), axis=0)

    ntx[0] = lax.fori_loop(0, 32, add_squares, jnp.zeros((8, 512), F32))
    norm_copies = [
        pltpu.make_async_remote_copy(
            src_ref=ntx.at[s], dst_ref=nrx.at[s], send_sem=n_send.at[s], recv_sem=n_recv.at[s],
            device_id=toward(d), device_id_type=MESH)
        for s, d in enumerate((XA, YA, XB, YB, "z"))
    ]
    norm_copies[0].start()

    load_s.wait()
    load_a.wait()
    inv[...] = 0.6 / (CENTER + inv[...])
    lane = lax.broadcasted_iota(jnp.int32, (64, 512), 1)
    first, last = lane == 0, lane == 511
    keep_down = jnp.where(slab > 0, 1.0, 0.0).astype(F32)
    keep_up = jnp.where(slab < 31, 1.0, 0.0).astype(F32)
    keep_west = jnp.where(blk > 0, 1.0, 0.0).astype(F32)
    keep_east = jnp.where(blk < 7, 1.0, 0.0).astype(F32)

    def sweep(pad, yrx, halos, store):
        for copy in halos:
            copy.wait_recv()
        for c in range(4):
            lanes = pl.ds(c * 128, 128)
            for row, base, keep in ((7, 0, keep_west), (72, 3, keep_east)):
                one = pl.ds(row, 1)
                pad[0, one, lanes] = yrx[base + 1, pl.ds(4 + c, 1), :] * keep
                pad[1, one, lanes] = yrx[base, pl.ds(c, 1), :] * keep
                pad[2, one, lanes] = yrx[base, pl.ds(4 + c, 1), :] * keep
                pad[3, one, lanes] = yrx[base + 2, pl.ds(c, 1), :] * keep

        def beside(z):
            v = pad[z, pl.ds(8, 64), :]
            s = pad[z, pl.ds(7, 64), :] + pad[z, pl.ds(9, 64), :]
            across = s * (1.0 / 6.0) + along_x(v * (1.0 / 6.0) + s * (1.0 / 12.0), first, last)
            return v, s, across

        low = beside(0)[2] * keep_down
        v0, s0, q0 = beside(1)
        v1, s1, q1 = beside(2)
        high = beside(3)[2] * keep_up
        e0 = low + q1 + along_x(s0, first, last) * (1.0 / 6.0)
        e1 = q0 + high + along_x(s1, first, last) * (1.0 / 6.0)
        store(0, 0.4 * v0 + inv[0] * (src[0] + e0))
        store(1, 0.4 * v1 + inv[1] * (src[1] + e1))

    def store_first(z, value):
        pad2[1 + z, pl.ds(8, 64), :] = value

    def store_second(z, value):
        relaxed[z] = value

    sweep(pad1, yrx1, halos1, store_first)
    for z in range(2):
        for c in range(4):
            lanes = pl.ds(c * 128, 128)
            ytx2[0, pl.ds(z * 4 + c, 1), :] = pad2[1 + z, pl.ds(8, 1), lanes]
            ytx2[1, pl.ds(z * 4 + c, 1), :] = pad2[1 + z, pl.ds(71, 1), lanes]
    for copy in halos2:
        copy.start()

    def add_in(part, stage, start, size):
        rows = pl.ds(start, size)
        prod[part, rows, :] += boxes[stage][part, rows, :]

    def norm_step(s):
        norm_copies[s].wait_recv()
        ntx[s + 1] = ntx[s] + nrx[s]
        norm_copies[s + 1].start()

    z_copies = [
        pltpu.make_async_remote_copy(
            src_ref=prod.at[part, pl.ds(pl.multiple_of((1 - my_z) * 32, 32), 32)], dst_ref=rx5.at[part],
            send_sem=rs_send.at[part, 4, 0], recv_sem=rs_recv.at[part, 4, 0],
            device_id=toward("z"), device_id_type=MESH)
        for part in range(4)
    ]

    for stage in range(1, 5):
        width = 1024 >> stage
        half = width // 2
        quarter = half // 2
        for part in range(4):
            copies[part, stage - 1, 0].wait_recv()
            if stage < 4:
                add_in(part, stage - 1, half + quarter, quarter)
                copies[part, stage, 0].start()
                add_in(part, stage - 1, half, quarter)
                copies[part, stage, 1].start()
            else:
                add_in(part, stage - 1, half, half)
        for part in range(4):
            copies[part, stage - 1, 1].wait_recv()
            add_in(part, stage - 1, 0, half)
            if stage == 4:
                z_copies[part].start()
        norm_step(stage - 1)
        if stage == 2:
            sweep(pad2, yrx2, halos2, store_second)

    norm_copies[4].wait_recv()
    sums = jnp.sum(ntx[4] + nrx[4], axis=0, keepdims=True)
    scale = 1.0 / jnp.sqrt(sums / NODES + 1e-06)
    own = pl.ds(pl.multiple_of(my_z * 32, 32), 32)
    for part in range(4):
        lanes = pl.ds(part * 128, 128)
        z_copies[part].wait_recv()
        flux[:, lanes] = (prod[part, own, :] + rx5[part]) * scale[:, part * 128:(part + 1) * 128]

    for copy in traces + halos1 + halos2 + norm_copies + z_copies + list(copies.values()):
        copy.wait_send()


def per_device(interior, sources, absorption, bem_panel, incident, node_cell, offset):
    any_space = pl.BlockSpec(memory_space=pl.ANY)
    vmem = pl.BlockSpec(memory_space=pltpu.VMEM)
    dma = pltpu.SemaphoreType.DMA
    return pl.pallas_call(
        kernel,
        out_shape=(
            jax.ShapeDtypeStruct((2, 64, 512), F32),
            jax.ShapeDtypeStruct((32, 512), F32),
        ),
        in_specs=[pl.BlockSpec(memory_space=pltpu.SMEM)] + [any_space] * 6,
        out_specs=(vmem, vmem),
        scratch_shapes=[
            pltpu.VMEM((4, 80, 512), F32),
            pltpu.VMEM((4, 80, 512), F32),
            pltpu.VMEM((2, 64, 512), F32),
            pltpu.VMEM((2, 64, 512), F32),
            pltpu.VMEM((2, 8, 128), F32),
            pltpu.VMEM((2, 8, 128), F32),
            pltpu.VMEM((6, 8, 128), F32),
            pltpu.VMEM((6, 8, 128), F32),
            pltpu.VMEM((32, 128), jnp.int32),
            pltpu.VMEM((8, 128), F32),
            pltpu.VMEM((8, 8, 128), F32),
            pltpu.VMEM((4096, 512), BF16),
            pltpu.VMEM((4096, 512), BF16),
            pltpu.VMEM((4, 4, 64, 4096), BF16),
            pltpu.VMEM((4, 1024, 128), F32),
            pltpu.VMEM((4, 512, 128), F32),
            pltpu.VMEM((4, 256, 128), F32),
            pltpu.VMEM((4, 128, 128), F32),
            pltpu.VMEM((4, 64, 128), F32),
            pltpu.VMEM((4, 32, 128), F32),
            pltpu.VMEM((5, 8, 512), F32),
            pltpu.VMEM((5, 8, 512), F32),
            dma((4,)),
            dma((4,)),
            dma((4, 4)),
            dma((2, 8)),
            dma((2, 8)),
            dma((8,)),
            dma((8,)),
            dma((4, 5, 2)),
            dma((4, 5, 2)),
            dma((5,)),
            dma((5,)),
        ],
        compiler_params=pltpu.CompilerParams(
            collective_id=0, has_side_effects=True, vmem_limit_bytes=56 * 1024 * 1024
        ),
        cost_estimate=pl.CostEstimate(flops=4300000000, bytes_accessed=14000000, transcendentals=0),
    )(offset, interior, sources, absorption, bem_panel, incident, node_cell.reshape(32, 128))


def solution(mesh):
    in_specs = (
        P("slab", "blk", None),
        P("slab", "blk", None),
        P("slab", "blk", None),
        P("blk", "slab"),
        P("slab", None),
        P("slab"),
        P(),
    )
    out_specs = (P("slab", "blk", None), P(("blk", "slab"), None))
    return jax.shard_map(
        per_device, mesh=mesh, in_specs=in_specs, out_specs=out_specs, check_vma=False
    )
```

```python
import jax
import jax.numpy as jnp
from jax import lax
from jax.experimental import pallas as pl
from jax.experimental.pallas import tpu as pltpu
from jax.sharding import PartitionSpec as P

F32 = jnp.float32
BF16 = jnp.bfloat16
MESH = pl.DeviceIdType.MESH
CENTER = 8.0 / 3.0


def flip(pos, low, high):
    if low:
        pos = pos + 1 - 2 * lax.rem(pos, 2)
    if high:
        pos = 3 - pos
    return pos


XA, XB, YA, YB = ("x", 1, 0), ("x", 0, 1), ("y", 1, 0), ("y", 0, 1)
XAB, YAB = ("x", 1, 1), ("y", 1, 1)
ORDERS = ((XA, YA, XB, YB), (YA, XA, YB, XB), (XB, YB, XA, YA), (YB, XB, YA, XA))
NODES = 131072.0


def along_x(w, first, last):
    n = w.shape[1]
    left = jnp.where(first, 0.0, pltpu.roll(w, 1, 1))
    right = jnp.where(last, 0.0, pltpu.roll(w, n - 1, 1))
    return left + right


def kernel(
    offset, interior, sources, absorption, bem, incident, cells,
    relaxed, flux,
    pad1, pad2, src, inv, ytx1, ytx2, yrx1, yrx2,
    cell_v, ttx, trx, pieces, inc_v, panel,
    prod, rx1, rx2, rx3, rx4, rx5, mtx, mrx,
    load_sem, inc_sem, panel_sem, halo_send, halo_recv,
    trace_send, trace_recv, rs_send, rs_recv, m_send, m_recv,
):
    slab, blk = lax.axis_index("slab"), lax.axis_index("blk")
    my_y, my_x, my_z = slab // 8, lax.rem(slab // 2, 4), lax.rem(slab, 2)

    def at(y, x, z):
        return y * 8 + x * 2 + z

    def toward(dim):
        if dim == "z":
            return (at(my_y, my_x, 1 - my_z), blk)
        axis, low, high = dim
        if axis == "x":
            return (at(my_y, flip(my_x, low, high), my_z), blk)
        return (at(flip(my_y, low, high), my_x, my_z), blk)

    up, down = lax.rem(slab + 1, 32), lax.rem(slab + 31, 32)
    east, west = lax.rem(blk + 1, 8), lax.rem(blk + 7, 8)

    core = pl.ds(8, 64)
    load_u = pltpu.make_async_copy(interior, pad1.at[pl.ds(1, 2), core], load_sem.at[0])
    load_c = pltpu.make_async_copy(cells, cell_v, load_sem.at[1])
    load_s = pltpu.make_async_copy(sources, src, load_sem.at[2])
    load_a = pltpu.make_async_copy(absorption, inv, load_sem.at[3])
    inc_load = pltpu.make_async_copy(incident, inc_v, inc_sem.at[0])
    panel_loads = {}
    order = sorted(((q, r) for q in range(4) for r in range(4)), key=lambda g: (-max(g), -g[0], -g[1]))
    for q, r in order:
        y = flip(my_y, q % 2, r % 2)
        x = flip(my_x, q // 2, r // 2)
        rows = pl.ds(pl.multiple_of(y * 256 + x * 64, 64), 64)
        panel_loads[q, r] = pltpu.make_async_copy(bem.at[rows], panel.at[q, r], panel_sem.at[q, r])
    load_u.start()
    load_c.start()
    inc_load.start()
    for group in order[:4]:
        panel_loads[group].start()

    partners = [(slab, lax.rem(blk + k, 8)) for k in range(1, 8)]
    partners += [toward(d) for d in (XA, XB, XAB, YA, YB, YAB, "z")]
    partners += [(up, blk), (down, blk), (up, east), (up, west), (down, east), (down, west)]
    barrier = pltpu.get_barrier_semaphore()
    for partner in partners:
        pl.semaphore_signal(barrier, inc=1, device_id=partner, device_id_type=MESH)

    load_u.wait()
    for z in range(2):
        for c in range(4):
            lanes = pl.ds(c * 128, 128)
            ytx1[0, pl.ds(z * 4 + c, 1), :] = pad1[1 + z, pl.ds(8, 1), lanes]
            ytx1[1, pl.ds(z * 4 + c, 1), :] = pad1[1 + z, pl.ds(71, 1), lanes]

    def halo_copies(sweep, pad, ytx, yrx):
        def copy(n, source, target, device):
            return pltpu.make_async_remote_copy(
                src_ref=source, dst_ref=target, send_sem=halo_send.at[sweep, n],
                recv_sem=halo_recv.at[sweep, n], device_id=device, device_id_type=MESH)
        return [
            copy(0, pad.at[2, core], pad.at[0, core], (up, blk)),
            copy(1, pad.at[1, core], pad.at[3, core], (down, blk)),
            copy(2, ytx.at[1], yrx.at[0], (slab, east)),
            copy(3, ytx.at[1], yrx.at[1], (up, east)),
            copy(4, ytx.at[1], yrx.at[2], (down, east)),
            copy(5, ytx.at[0], yrx.at[3], (slab, west)),
            copy(6, ytx.at[0], yrx.at[4], (up, west)),
            copy(7, ytx.at[0], yrx.at[5], (down, west)),
        ]

    halos1 = halo_copies(0, pad1, ytx1, yrx1)
    halos2 = halo_copies(1, pad2, ytx2, yrx2)
    pl.semaphore_wait(barrier, len(partners))
    for copy in halos1:
        copy.start()

    for group in order[4:]:
        panel_loads[group].start()
    load_s.start()
    load_a.start()

    load_c.wait()
    y_index = lax.broadcasted_iota(jnp.int32, (64, 128), 0) * 2
    totals = [jnp.zeros((64, 128), F32)] * 4
    for z in range(2):
        for side in range(2):
            face = jnp.broadcast_to(pad1[1 + z, pl.ds(8, 64), pl.ds(511 * side, 1)], (64, 128))
            for c in range(4):
                cell = cell_v[pl.ds(blk * 4 + c, 1), :]
                totals[c] += jnp.where(cell == y_index + (z * 128 + side), face, 0.0)
    found = [jnp.sum(total, axis=0, keepdims=True) for total in totals]
    for c in range(4):
        ttx[pl.ds(c, 1), :] = found[c]

    inc_load.wait()
    turned = jnp.concatenate(found + [jnp.zeros((124, 128), F32)], axis=0).T
    squares = jnp.zeros((8, 512), F32)
    for c in range(4):
        rows = pl.ds(pl.multiple_of(blk * 512 + c * 128, 128), 128)
        column = lax.slice(turned, (0, c), (128, c + 1))
        x = (inc_v[rows, :].astype(F32) + column).astype(BF16).astype(F32)
        squares += jnp.sum((x * x).reshape(16, 8, 512), axis=0)
    squares = jnp.sum(squares, axis=0, keepdims=True)
    for c in range(4):
        ttx[pl.ds(4 + c, 1), :] = squares[:, c * 128:(c + 1) * 128]
    trx[0] = ttx[...]

    traces = []
    for k in range(1, 8):
        traces.append(pltpu.make_async_remote_copy(
            src_ref=ttx, dst_ref=trx.at[k], send_sem=trace_send.at[k], recv_sem=trace_recv.at[k],
            device_id=(slab, lax.rem(blk + k, 8)), device_id_type=MESH))
        traces[-1].start()

    wanted = offset[0] // 4096 + blk // 4
    hit = jnp.full((8, 128), wanted, jnp.int32) == jnp.full((8, 128), slab, jnp.int32)
    coef = jnp.where(hit, 0.5, 0.0).astype(F32)[0:1, 0:1]
    jump_base = lax.rem(blk, 4) * 1024

    boxes = (rx1, rx2, rx3, rx4)
    chunks = (2, 2, 2, 1)
    waited = set()

    def arrived(part, stage, chunk):
        if chunk < chunks[stage] and (part, stage, chunk) not in waited:
            waited.add((part, stage, chunk))
            copies[part, stage, chunk].wait_recv()

    def rs_copy(part, stage, chunk):
        size = 512 >> stage
        piece = size // chunks[stage]
        start = size - (chunk + 1) * piece
        return pltpu.make_async_remote_copy(
            src_ref=prod.at[part, pl.ds(size + start, piece)],
            dst_ref=boxes[stage].at[part, pl.ds(start, piece)],
            send_sem=rs_send.at[part, stage, chunk], recv_sem=rs_recv.at[part, stage, chunk],
            device_id=toward(ORDERS[part][stage]), device_id_type=MESH)

    copies = {(p, s, c): rs_copy(p, s, c) for p in range(4) for s in range(4) for c in range(chunks[s])}

    def swapped(q):
        return (q % 2) * 2 + q // 2

    def unit(pair, q):
        for r in range(4):
            copy = panel_loads.pop((q, r) if pair == 0 else (r, q), None)
            if copy is not None:
                copy.wait()
        lhs = panel[q] if pair == 0 else panel[:, q]
        cols = pl.ds(pair * 256, 256)
        out = jnp.dot(lhs.reshape(256, 4096), inc_v[:, cols], preferred_element_type=F32)
        for r in range(4):
            qa, qb = (q, r) if pair == 0 else (r, q)
            y = flip(my_y, qa % 2, qb % 2)
            x = flip(my_x, qa // 2, qb // 2)
            rows = pl.ds(pl.multiple_of(jump_base + y * 256 + x * 64, 64), 64)
            piece = out[r * 64:(r + 1) * 64] + coef * inc_v[rows, cols].astype(F32)
            prod[pair * 2, pl.ds(q * 256 + r * 64, 64), :] = piece[:, :128]
            prod[pair * 2 + 1, pl.ds(swapped(q) * 256 + swapped(r) * 64, 64), :] = piece[:, 128:]

    for pair in range(2):
        unit(pair, 3)
        copies[pair * 2, 0, 0].start()
        copies[pair * 2 + 1, 0, 0].start()
    for pair in range(2):
        unit(pair, 2)
        copies[pair * 2, 0, 1].start()
    for pair in range(2):
        unit(pair, 1)
        copies[pair * 2 + 1, 0, 1].start()
    for pair in range(2):
        unit(pair, 0)

    lane = lax.broadcasted_iota(jnp.int32, (64, 512), 1)
    first, last = lane == 0, lane == 511
    keep_down = jnp.where(slab > 0, 1.0, 0.0).astype(F32)
    keep_up = jnp.where(slab < 31, 1.0, 0.0).astype(F32)
    keep_west = jnp.where(blk > 0, 1.0, 0.0).astype(F32)
    keep_east = jnp.where(blk < 7, 1.0, 0.0).astype(F32)

    def sweep(pad, yrx, halos, store):
        for copy in halos:
            copy.wait_recv()
        for c in range(4):
            lanes = pl.ds(c * 128, 128)
            for row, base, keep in ((7, 0, keep_west), (72, 3, keep_east)):
                one = pl.ds(row, 1)
                pad[0, one, lanes] = yrx[base + 1, pl.ds(4 + c, 1), :] * keep
                pad[1, one, lanes] = yrx[base, pl.ds(c, 1), :] * keep
                pad[2, one, lanes] = yrx[base, pl.ds(4 + c, 1), :] * keep
                pad[3, one, lanes] = yrx[base + 2, pl.ds(c, 1), :] * keep

        def beside(z):
            v = pad[z, pl.ds(8, 64), :]
            s = pad[z, pl.ds(7, 64), :] + pad[z, pl.ds(9, 64), :]
            across = s * (1.0 / 6.0) + along_x(v * (1.0 / 6.0) + s * (1.0 / 12.0), first, last)
            return v, s, across

        low = beside(0)[2] * keep_down
        v0, s0, q0 = beside(1)
        v1, s1, q1 = beside(2)
        high = beside(3)[2] * keep_up
        e0 = low + q1 + along_x(s0, first, last) * (1.0 / 6.0)
        e1 = q0 + high + along_x(s1, first, last) * (1.0 / 6.0)
        store(0, 0.4 * v0 + inv[0] * (src[0] + e0))
        store(1, 0.4 * v1 + inv[1] * (src[1] + e1))

    def sweep_first():
        load_s.wait()
        load_a.wait()
        inv[...] = 0.6 / (CENTER + inv[...])

        def store(z, value):
            pad2[1 + z, pl.ds(8, 64), :] = value

        sweep(pad1, yrx1, halos1, store)
        for z in range(2):
            for c in range(4):
                lanes = pl.ds(c * 128, 128)
                ytx2[0, pl.ds(z * 4 + c, 1), :] = pad2[1 + z, pl.ds(8, 1), lanes]
                ytx2[1, pl.ds(z * 4 + c, 1), :] = pad2[1 + z, pl.ds(71, 1), lanes]
        for copy in halos2:
            copy.start()

    def sweep_second():
        def store(z, value):
            relaxed[z] = value

        sweep(pad2, yrx2, halos2, store)

    groups = ([XA, XB, XAB], [YA, YB, YAB], ["z"])
    sends = [
        [
            pltpu.make_async_remote_copy(
                src_ref=mtx.at[s], dst_ref=mrx.at[s, n], send_sem=m_send.at[s, n], recv_sem=m_recv.at[s, n],
                device_id=toward(d), device_id_type=MESH)
            for n, d in enumerate(group)
        ]
        for s, group in enumerate(groups)
    ]

    def trace_products():
        for copy in traces:
            copy.wait_recv()
        pieces[...] = jnp.zeros((16, 4096), F32)
        squares = trx[0, pl.ds(4, 4), :]
        for k in range(1, 8):
            squares += trx[k, pl.ds(4, 4), :]
        for k in range(8):
            base = lax.rem(blk + 8 - k, 8) * 512
            for c in range(4):
                lanes = pl.ds(pl.multiple_of(base + c * 128, 128), 128)
                rest = trx[k, pl.ds(c, 1), :]
                for n in range(3):
                    piece = rest.astype(BF16).astype(F32)
                    pieces[pl.ds(n, 1), lanes] = piece
                    rest = rest - piece
        spread = lax.dot_general(
            pieces[...].astype(BF16), panel[...].reshape(1024, 4096), (((1,), (1,)), ((), ())),
            preferred_element_type=F32)
        row = spread[0:1] + spread[1:2] + spread[2:3]
        mtx[0] = jnp.zeros((24, 128), F32)
        mtx[0, pl.ds(0, 4), :] = squares
        for q in range(4):
            for r in range(4):
                y = flip(my_y, q % 2, r % 2)
                x = flip(my_x, q // 2, r // 2)
                g = q * 4 + r
                mtx[0, pl.ds(8 + y * 4 + x, 1), pl.ds(0, 64)] = row[:, g * 64:(g + 1) * 64]
        for g in range(16):
            k = lax.rem(blk + 8 - (lax.rem(blk, 4) * 2 + g // 8), 8)
            there = trx[k, pl.ds(g % 8 // 2, 1), :][:, g % 2 * 64:g % 2 * 64 + 64]
            mtx[0, pl.ds(8 + g, 1), pl.ds(0, 64)] += coef * there
        for copy in sends[0]:
            copy.start()

    def message_sum(s):
        total = mtx[s]
        for n, copy in enumerate(sends[s]):
            copy.wait_recv()
            total += mrx[s, n]
        return total

    def message_step(s):
        mtx[s] = message_sum(s - 1)
        for copy in sends[s]:
            copy.start()

    def added(part, rows, stages):
        total = prod[part, rows, :]
        for stage in range(stages):
            total += boxes[stage][part, rows, :]
        return total

    def halving(stage):
        size = 512 >> stage
        for part in range(4):
            if stage >= 2:
                arrived(part, stage - 2, 1)
            arrived(part, stage - 1, 0)
            piece = size // chunks[stage]
            for chunk in range(chunks[stage]):
                rows = pl.ds(2 * size - (chunk + 1) * piece, piece)
                prod[part, rows, :] = added(part, rows, stage)
                copies[part, stage, chunk].start()

    own = pl.ds(pl.multiple_of(my_z * 32, 32), 32)
    other = pl.ds(pl.multiple_of((1 - my_z) * 32, 32), 32)
    z_copies = [
        pltpu.make_async_remote_copy(
            src_ref=prod.at[part, other], dst_ref=rx5.at[part],
            send_sem=rs_send.at[part, 4, 0], recv_sem=rs_recv.at[part, 4, 0],
            device_id=toward("z"), device_id_type=MESH)
        for part in range(4)
    ]

    def last_halving():
        for part in range(4):
            arrived(part, 2, 1)
            arrived(part, 3, 0)
            arrived(part, 3, 1)
            prod[part, other, :] = added(part, other, 4)
            z_copies[part].start()

    def finish():
        message = message_sum(2)
        mtx[3] = message
        row = mtx[3, pl.ds(8 + my_y * 4 + my_x, 1), :]
        here = lax.broadcasted_iota(jnp.int32, (32, 128), 1) == (
            lax.broadcasted_iota(jnp.int32, (32, 128), 0) + 32 * my_z)
        column = jnp.sum(jnp.where(here, row, 0.0), axis=1, keepdims=True)
        for part in range(4):
            scale = 1.0 / jnp.sqrt(message[part:part + 1] / NODES + 1e-06)
            z_copies[part].wait_recv()
            flux[:, pl.ds(part * 128, 128)] = (added(part, own, 4) + rx5[part] + column) * scale

    halving(1)
    trace_products()
    sweep_first()
    halving(2)
    message_step(1)
    halving(3)
    message_step(2)
    last_halving()
    sweep_second()
    finish()

    for copy in traces + halos1 + halos2 + sum(sends, []) + z_copies + list(copies.values()):
        copy.wait_send()


def hand_over(relaxed, flux, relaxed_out, flux_out):
    relaxed_out[...] = relaxed[...]
    flux_out[...] = flux[...]


def per_device(interior, sources, absorption, bem_panel, incident, node_cell, offset):
    any_space = pl.BlockSpec(memory_space=pl.ANY)
    vmem = pl.BlockSpec(memory_space=pltpu.VMEM)
    dma = pltpu.SemaphoreType.DMA
    shapes = (
        jax.ShapeDtypeStruct((2, 64, 512), F32),
        jax.ShapeDtypeStruct((32, 512), F32),
    )
    results = pl.pallas_call(
        kernel,
        out_shape=shapes,
        in_specs=[pl.BlockSpec(memory_space=pltpu.SMEM)] + [any_space] * 6,
        out_specs=(vmem, vmem),
        scratch_shapes=[
            pltpu.VMEM((4, 80, 512), F32),
            pltpu.VMEM((4, 80, 512), F32),
            pltpu.VMEM((2, 64, 512), F32),
            pltpu.VMEM((2, 64, 512), F32),
            pltpu.VMEM((2, 8, 128), F32),
            pltpu.VMEM((2, 8, 128), F32),
            pltpu.VMEM((6, 8, 128), F32),
            pltpu.VMEM((6, 8, 128), F32),
            pltpu.VMEM((32, 128), jnp.int32),
            pltpu.VMEM((8, 128), F32),
            pltpu.VMEM((8, 8, 128), F32),
            pltpu.VMEM((16, 4096), F32),
            pltpu.VMEM((4096, 512), BF16),
            pltpu.VMEM((4, 4, 64, 4096), BF16),
            pltpu.VMEM((4, 1024, 128), F32),
            pltpu.VMEM((4, 512, 128), F32),
            pltpu.VMEM((4, 256, 128), F32),
            pltpu.VMEM((4, 128, 128), F32),
            pltpu.VMEM((4, 64, 128), F32),
            pltpu.VMEM((4, 32, 128), F32),
            pltpu.VMEM((4, 24, 128), F32),
            pltpu.VMEM((3, 3, 24, 128), F32),
            dma((4,)),
            dma((4,)),
            dma((4, 4)),
            dma((2, 8)),
            dma((2, 8)),
            dma((8,)),
            dma((8,)),
            dma((4, 5, 2)),
            dma((4, 5, 2)),
            dma((3, 3)),
            dma((3, 3)),
        ],
        compiler_params=pltpu.CompilerParams(
            collective_id=0, has_side_effects=True, vmem_limit_bytes=56 * 1024 * 1024
        ),
        cost_estimate=pl.CostEstimate(flops=4300000000, bytes_accessed=14000000, transcendentals=0),
    )(offset, interior, sources, absorption, bem_panel, incident, node_cell.reshape(32, 128))
    return pl.pallas_call(
        hand_over,
        out_shape=shapes,
        in_specs=[vmem] * 2,
        out_specs=(vmem,) * 2,
    )(*results)


def solution(mesh):
    in_specs = (
        P("slab", "blk", None),
        P("slab", "blk", None),
        P("slab", "blk", None),
        P("blk", "slab"),
        P("slab", None),
        P("slab"),
        P(),
    )
    out_specs = (P("slab", "blk", None), P(("blk", "slab"), None))
    return jax.shard_map(
        per_device, mesh=mesh, in_specs=in_specs, out_specs=out_specs, check_vma=False
    )
```

```python
import jax
import jax.numpy as jnp
from jax import lax
from jax.experimental import pallas as pl
from jax.experimental.pallas import tpu as pltpu
from jax.sharding import PartitionSpec as P

F32 = jnp.float32
BF16 = jnp.bfloat16
MESH = pl.DeviceIdType.MESH
CENTER = 8.0 / 3.0


def flip(pos, low, high):
    if low:
        pos = pos + 1 - 2 * lax.rem(pos, 2)
    if high:
        pos = 3 - pos
    return pos


XA, XB, YA, YB = ("x", 1, 0), ("x", 0, 1), ("y", 1, 0), ("y", 0, 1)
XAB, YAB = ("x", 1, 1), ("y", 1, 1)
ORDERS = ((XA, YA, XB, YB), (YA, XA, YB, XB), (XB, YB, XA, YA), (YB, XB, YA, XA))
NODES = 131072.0


def along_x(w, first, last):
    n = w.shape[1]
    left = jnp.where(first, 0.0, pltpu.roll(w, 1, 1))
    right = jnp.where(last, 0.0, pltpu.roll(w, n - 1, 1))
    return left + right


def kernel(
    offset, interior, sources, absorption, bem, incident, cells,
    relaxed_out, flux_out, relaxed, flux,
    pad1, pad2, src, inv, ytx1, ytx2, yrx1, yrx2,
    cell_v, ttx, trx, pieces, inc_v, panel,
    prod, rx1, rx2, rx3, rx4, rx5, mtx, mrx,
    out_sem, load_sem, inc_sem, panel_sem, halo_send, halo_recv,
    trace_send, trace_recv, rs_send, rs_recv, m_send, m_recv,
):
    slab, blk = lax.axis_index("slab"), lax.axis_index("blk")
    my_y, my_x, my_z = slab // 8, lax.rem(slab // 2, 4), lax.rem(slab, 2)

    def at(y, x, z):
        return y * 8 + x * 2 + z

    def toward(dim):
        if dim == "z":
            return (at(my_y, my_x, 1 - my_z), blk)
        axis, low, high = dim
        if axis == "x":
            return (at(my_y, flip(my_x, low, high), my_z), blk)
        return (at(flip(my_y, low, high), my_x, my_z), blk)

    up, down = lax.rem(slab + 1, 32), lax.rem(slab + 31, 32)
    east, west = lax.rem(blk + 1, 8), lax.rem(blk + 7, 8)

    core = pl.ds(8, 64)
    load_u = pltpu.make_async_copy(interior, pad1.at[pl.ds(1, 2), core], load_sem.at[0])
    load_c = pltpu.make_async_copy(cells, cell_v, load_sem.at[1])
    load_s = pltpu.make_async_copy(sources, src, load_sem.at[2])
    load_a = pltpu.make_async_copy(absorption, inv, load_sem.at[3])
    inc_load = pltpu.make_async_copy(incident, inc_v, inc_sem.at[0])
    panel_loads = {}
    order = sorted(((q, r) for q in range(4) for r in range(4)), key=lambda g: (-max(g), -g[0], -g[1]))
    for q, r in order:
        y = flip(my_y, q % 2, r % 2)
        x = flip(my_x, q // 2, r // 2)
        rows = pl.ds(pl.multiple_of(y * 256 + x * 64, 64), 64)
        panel_loads[q, r] = pltpu.make_async_copy(bem.at[rows], panel.at[q, r], panel_sem.at[q, r])
    load_u.start()
    load_c.start()
    inc_load.start()
    for group in order[:4]:
        panel_loads[group].start()

    partners = [(slab, lax.rem(blk + k, 8)) for k in range(1, 8)]
    partners += [toward(d) for d in (XA, XB, XAB, YA, YB, YAB, "z")]
    partners += [(up, blk), (down, blk), (up, east), (up, west), (down, east), (down, west)]
    barrier = pltpu.get_barrier_semaphore()
    for partner in partners:
        pl.semaphore_signal(barrier, inc=1, device_id=partner, device_id_type=MESH)

    load_u.wait()
    for z in range(2):
        for c in range(4):
            lanes = pl.ds(c * 128, 128)
            ytx1[0, pl.ds(z * 4 + c, 1), :] = pad1[1 + z, pl.ds(8, 1), lanes]
            ytx1[1, pl.ds(z * 4 + c, 1), :] = pad1[1 + z, pl.ds(71, 1), lanes]

    def halo_copies(sweep, pad, ytx, yrx):
        def copy(n, source, target, device):
            return pltpu.make_async_remote_copy(
                src_ref=source, dst_ref=target, send_sem=halo_send.at[sweep, n],
                recv_sem=halo_recv.at[sweep, n], device_id=device, device_id_type=MESH)
        return [
            copy(0, pad.at[2, core], pad.at[0, core], (up, blk)),
            copy(1, pad.at[1, core], pad.at[3, core], (down, blk)),
            copy(2, ytx.at[1], yrx.at[0], (slab, east)),
            copy(3, ytx.at[1], yrx.at[1], (up, east)),
            copy(4, ytx.at[1], yrx.at[2], (down, east)),
            copy(5, ytx.at[0], yrx.at[3], (slab, west)),
            copy(6, ytx.at[0], yrx.at[4], (up, west)),
            copy(7, ytx.at[0], yrx.at[5], (down, west)),
        ]

    halos1 = halo_copies(0, pad1, ytx1, yrx1)
    halos2 = halo_copies(1, pad2, ytx2, yrx2)
    pl.semaphore_wait(barrier, len(partners))
    def start_planes(halos, near):
        @pl.when(my_z == (0 if near else 1))
        def _():
            halos[0].start()

        @pl.when(my_z == (1 if near else 0))
        def _():
            halos[1].start()

    for copy in halos1[2:]:
        copy.start()
    start_planes(halos1, False)
    start_planes(halos1, True)

    for group in order[4:]:
        panel_loads[group].start()
    load_s.start()
    load_a.start()

    wanted = offset[0] // 4096 + blk // 4
    hit = jnp.full((8, 128), wanted, jnp.int32) == jnp.full((8, 128), slab, jnp.int32)
    coef = jnp.where(hit, 0.5, 0.0).astype(F32)[0:1, 0:1]
    jump_base = lax.rem(blk, 4) * 1024

    boxes = (rx1, rx2, rx3, rx4)
    chunks = (2, 2, 2, 1)
    waited = set()

    def arrived(part, stage, chunk):
        if chunk < chunks[stage] and (part, stage, chunk) not in waited:
            waited.add((part, stage, chunk))
            copies[part, stage, chunk].wait_recv()

    def rs_copy(part, stage, chunk):
        size = 512 >> stage
        piece = size // chunks[stage]
        start = size - (chunk + 1) * piece
        return pltpu.make_async_remote_copy(
            src_ref=prod.at[part, pl.ds(size + start, piece)],
            dst_ref=boxes[stage].at[part, pl.ds(start, piece)],
            send_sem=rs_send.at[part, stage, chunk], recv_sem=rs_recv.at[part, stage, chunk],
            device_id=toward(ORDERS[part][stage]), device_id_type=MESH)

    copies = {(p, s, c): rs_copy(p, s, c) for p in range(4) for s in range(4) for c in range(chunks[s])}

    def swapped(q):
        return (q % 2) * 2 + q // 2

    def unit(pair, q):
        for r in range(4):
            copy = panel_loads.pop((q, r) if pair == 0 else (r, q), None)
            if copy is not None:
                copy.wait()
        lhs = panel[q] if pair == 0 else panel[:, q]
        cols = pl.ds(pair * 256, 256)
        out = jnp.dot(lhs.reshape(256, 4096), inc_v[:, cols], preferred_element_type=F32)
        for r in range(4):
            qa, qb = (q, r) if pair == 0 else (r, q)
            y = flip(my_y, qa % 2, qb % 2)
            x = flip(my_x, qa // 2, qb // 2)
            rows = pl.ds(pl.multiple_of(jump_base + y * 256 + x * 64, 64), 64)
            piece = out[r * 64:(r + 1) * 64] + coef * inc_v[rows, cols].astype(F32)
            prod[pair * 2, pl.ds(q * 256 + r * 64, 64), :] = piece[:, :128]
            prod[pair * 2 + 1, pl.ds(swapped(q) * 256 + swapped(r) * 64, 64), :] = piece[:, 128:]

    def first_units(pair):
        unit(pair, 3)
        copies[pair * 2, 0, 0].start()
        copies[pair * 2 + 1, 0, 0].start()

    load_c.wait()
    y_index = lax.broadcasted_iota(jnp.int32, (64, 128), 0) * 2
    totals = [jnp.zeros((64, 128), F32)] * 4
    for z in range(2):
        for side in range(2):
            face = jnp.broadcast_to(pad1[1 + z, pl.ds(8, 64), pl.ds(511 * side, 1)], (64, 128))
            for c in range(4):
                cell = cell_v[pl.ds(blk * 4 + c, 1), :]
                totals[c] += jnp.where(cell == y_index + (z * 128 + side), face, 0.0)
    found = [jnp.sum(total, axis=0, keepdims=True) for total in totals]
    for c in range(4):
        ttx[pl.ds(c, 1), :] = found[c]

    inc_load.wait()
    turned = jnp.concatenate(found + [jnp.zeros((124, 128), F32)], axis=0).T
    squares = jnp.zeros((8, 512), F32)
    for c in range(4):
        rows = pl.ds(pl.multiple_of(blk * 512 + c * 128, 128), 128)
        column = lax.slice(turned, (0, c), (128, c + 1))
        x = (inc_v[rows, :].astype(F32) + column).astype(BF16).astype(F32)
        squares += jnp.sum((x * x).reshape(16, 8, 512), axis=0)
    squares = jnp.sum(squares, axis=0, keepdims=True)
    for c in range(4):
        ttx[pl.ds(4 + c, 1), :] = squares[:, c * 128:(c + 1) * 128]
    trx[0] = ttx[...]

    traces = []
    for k in range(1, 8):
        traces.append(pltpu.make_async_remote_copy(
            src_ref=ttx, dst_ref=trx.at[k], send_sem=trace_send.at[k], recv_sem=trace_recv.at[k],
            device_id=(slab, lax.rem(blk + k, 8)), device_id_type=MESH))
        traces[-1].start()

    for pair in range(2):
        first_units(pair)
    for pair in range(2):
        unit(pair, 2)
        copies[pair * 2, 0, 1].start()
    for pair in range(2):
        unit(pair, 1)
        copies[pair * 2 + 1, 0, 1].start()
    for pair in range(2):
        unit(pair, 0)

    lane = lax.broadcasted_iota(jnp.int32, (64, 512), 1)
    first, last = lane == 0, lane == 511
    keep_down = jnp.where(slab > 0, 1.0, 0.0).astype(F32)
    keep_up = jnp.where(slab < 31, 1.0, 0.0).astype(F32)
    keep_west = jnp.where(blk > 0, 1.0, 0.0).astype(F32)
    keep_east = jnp.where(blk < 7, 1.0, 0.0).astype(F32)

    def sweep(pad, yrx, halos, store):
        for copy in halos:
            copy.wait_recv()
        for c in range(4):
            lanes = pl.ds(c * 128, 128)
            for row, base, keep in ((7, 0, keep_west), (72, 3, keep_east)):
                one = pl.ds(row, 1)
                pad[0, one, lanes] = yrx[base + 1, pl.ds(4 + c, 1), :] * keep
                pad[1, one, lanes] = yrx[base, pl.ds(c, 1), :] * keep
                pad[2, one, lanes] = yrx[base, pl.ds(4 + c, 1), :] * keep
                pad[3, one, lanes] = yrx[base + 2, pl.ds(c, 1), :] * keep

        def beside(z):
            v = pad[z, pl.ds(8, 64), :]
            s = pad[z, pl.ds(7, 64), :] + pad[z, pl.ds(9, 64), :]
            across = s * (1.0 / 6.0) + along_x(v * (1.0 / 6.0) + s * (1.0 / 12.0), first, last)
            return v, s, across

        low = beside(0)[2] * keep_down
        v0, s0, q0 = beside(1)
        v1, s1, q1 = beside(2)
        high = beside(3)[2] * keep_up
        e0 = low + q1 + along_x(s0, first, last) * (1.0 / 6.0)
        e1 = q0 + high + along_x(s1, first, last) * (1.0 / 6.0)
        store(0, 0.4 * v0 + inv[0] * (src[0] + e0))
        store(1, 0.4 * v1 + inv[1] * (src[1] + e1))

    def sweep_first():
        load_s.wait()
        load_a.wait()
        inv[...] = 0.6 / (CENTER + inv[...])

        def store(z, value):
            pad2[1 + z, pl.ds(8, 64), :] = value

        sweep(pad1, yrx1, halos1, store)
        for z in range(2):
            for c in range(4):
                lanes = pl.ds(c * 128, 128)
                ytx2[0, pl.ds(z * 4 + c, 1), :] = pad2[1 + z, pl.ds(8, 1), lanes]
                ytx2[1, pl.ds(z * 4 + c, 1), :] = pad2[1 + z, pl.ds(71, 1), lanes]
        for copy in halos2[2:]:
            copy.start()
        start_planes(halos2, False)
        start_planes(halos2, True)

    relaxed_copy = pltpu.make_async_copy(relaxed, relaxed_out, out_sem.at[0])
    flux_copy = pltpu.make_async_copy(flux, flux_out, out_sem.at[1])

    def sweep_second():
        def store(z, value):
            relaxed[z] = value

        sweep(pad2, yrx2, halos2, store)
        relaxed_copy.start()

    groups = ([XA, XB, XAB], [YA, YB, YAB], ["z"])
    sends = [
        [
            pltpu.make_async_remote_copy(
                src_ref=mtx.at[s], dst_ref=mrx.at[s, n], send_sem=m_send.at[s, n], recv_sem=m_recv.at[s, n],
                device_id=toward(d), device_id_type=MESH)
            for n, d in enumerate(group)
        ]
        for s, group in enumerate(groups)
    ]

    def trace_products():
        for copy in traces:
            copy.wait_recv()
        pieces[...] = jnp.zeros((16, 4096), F32)
        squares = trx[0, pl.ds(4, 4), :]
        for k in range(1, 8):
            squares += trx[k, pl.ds(4, 4), :]
        for k in range(8):
            base = lax.rem(blk + 8 - k, 8) * 512
            for c in range(4):
                lanes = pl.ds(pl.multiple_of(base + c * 128, 128), 128)
                rest = trx[k, pl.ds(c, 1), :]
                for n in range(3):
                    piece = rest.astype(BF16).astype(F32)
                    pieces[pl.ds(n, 1), lanes] = piece
                    rest = rest - piece
        spread = lax.dot_general(
            pieces[...].astype(BF16), panel[...].reshape(1024, 4096), (((1,), (1,)), ((), ())),
            preferred_element_type=F32)
        row = spread[0:1] + spread[1:2] + spread[2:3]
        mtx[0] = jnp.zeros((24, 128), F32)
        mtx[0, pl.ds(0, 4), :] = squares
        for q in range(4):
            for r in range(4):
                y = flip(my_y, q % 2, r % 2)
                x = flip(my_x, q // 2, r // 2)
                g = q * 4 + r
                mtx[0, pl.ds(8 + y * 4 + x, 1), pl.ds(0, 64)] = row[:, g * 64:(g + 1) * 64]
        for g in range(16):
            k = lax.rem(blk + 8 - (lax.rem(blk, 4) * 2 + g // 8), 8)
            there = trx[k, pl.ds(g % 8 // 2, 1), :][:, g % 2 * 64:g % 2 * 64 + 64]
            mtx[0, pl.ds(8 + g, 1), pl.ds(0, 64)] += coef * there
        for copy in sends[0]:
            copy.start()

    def message_sum(s):
        total = mtx[s]
        for n, copy in enumerate(sends[s]):
            copy.wait_recv()
            total += mrx[s, n]
        return total

    def message_step(s):
        mtx[s] = message_sum(s - 1)
        for copy in sends[s]:
            copy.start()

    def added(part, rows, stages):
        total = prod[part, rows, :]
        for stage in range(stages):
            total += boxes[stage][part, rows, :]
        return total

    def halving(stage):
        size = 512 >> stage
        for part in range(4):
            if stage >= 2:
                arrived(part, stage - 2, 1)
            arrived(part, stage - 1, 0)
            piece = size // chunks[stage]
            for chunk in range(chunks[stage]):
                rows = pl.ds(2 * size - (chunk + 1) * piece, piece)
                prod[part, rows, :] = added(part, rows, stage)
                copies[part, stage, chunk].start()

    own = pl.ds(pl.multiple_of(my_z * 32, 32), 32)
    other = pl.ds(pl.multiple_of((1 - my_z) * 32, 32), 32)
    z_copies = [
        pltpu.make_async_remote_copy(
            src_ref=prod.at[part, other], dst_ref=rx5.at[part],
            send_sem=rs_send.at[part, 4, 0], recv_sem=rs_recv.at[part, 4, 0],
            device_id=toward("z"), device_id_type=MESH)
        for part in range(4)
    ]

    def last_halving():
        for part in range(4):
            arrived(part, 2, 1)
            arrived(part, 3, 0)
            arrived(part, 3, 1)
            prod[part, other, :] = added(part, other, 4)
            z_copies[part].start()

    def finish():
        message = message_sum(2)
        mtx[3] = message
        row = mtx[3, pl.ds(8 + my_y * 4 + my_x, 1), :]
        here = lax.broadcasted_iota(jnp.int32, (32, 128), 1) == (
            lax.broadcasted_iota(jnp.int32, (32, 128), 0) + 32 * my_z)
        column = jnp.sum(jnp.where(here, row, 0.0), axis=1, keepdims=True)
        for part in range(4):
            scale = 1.0 / jnp.sqrt(message[part:part + 1] / NODES + 1e-06)
            z_copies[part].wait_recv()
            flux[:, pl.ds(part * 128, 128)] = (added(part, own, 4) + rx5[part] + column) * scale
        flux_copy.start()

    def sent(group):
        for copy in group:
            copy.wait_send()

    def stage_copies(stage):
        return [copies[p, stage, c] for p in range(4) for c in range(chunks[stage])]

    halving(1)
    trace_products()
    sweep_first()
    halving(2)
    sent(traces + halos1 + stage_copies(0))
    message_step(1)
    halving(3)
    sent(sends[0] + stage_copies(1))
    message_step(2)
    last_halving()
    sent(sends[1] + halos2 + stage_copies(2))
    sweep_second()
    finish()

    sent(sends[2] + stage_copies(3) + z_copies)
    relaxed_copy.wait()
    flux_copy.wait()


def hand_over(relaxed, flux, relaxed_out, flux_out):
    relaxed_out[...] = relaxed[...]
    flux_out[...] = flux[...]


def per_device(interior, sources, absorption, bem_panel, incident, node_cell, offset):
    any_space = pl.BlockSpec(memory_space=pl.ANY)
    vmem = pl.BlockSpec(memory_space=pltpu.VMEM)
    dma = pltpu.SemaphoreType.DMA
    shapes = (
        jax.ShapeDtypeStruct((2, 64, 512), F32),
        jax.ShapeDtypeStruct((32, 512), F32),
    )
    results = pl.pallas_call(
        kernel,
        out_shape=shapes,
        in_specs=[pl.BlockSpec(memory_space=pltpu.SMEM)] + [any_space] * 6,
        out_specs=(any_space, any_space),
        scratch_shapes=[
            pltpu.VMEM((2, 64, 512), F32),
            pltpu.VMEM((32, 512), F32),
            pltpu.VMEM((4, 80, 512), F32),
            pltpu.VMEM((4, 80, 512), F32),
            pltpu.VMEM((2, 64, 512), F32),
            pltpu.VMEM((2, 64, 512), F32),
            pltpu.VMEM((2, 8, 128), F32),
            pltpu.VMEM((2, 8, 128), F32),
            pltpu.VMEM((6, 8, 128), F32),
            pltpu.VMEM((6, 8, 128), F32),
            pltpu.VMEM((32, 128), jnp.int32),
            pltpu.VMEM((8, 128), F32),
            pltpu.VMEM((8, 8, 128), F32),
            pltpu.VMEM((16, 4096), F32),
            pltpu.VMEM((4096, 512), BF16),
            pltpu.VMEM((4, 4, 64, 4096), BF16),
            pltpu.VMEM((4, 1024, 128), F32),
            pltpu.VMEM((4, 512, 128), F32),
            pltpu.VMEM((4, 256, 128), F32),
            pltpu.VMEM((4, 128, 128), F32),
            pltpu.VMEM((4, 64, 128), F32),
            pltpu.VMEM((4, 32, 128), F32),
            pltpu.VMEM((4, 24, 128), F32),
            pltpu.VMEM((3, 3, 24, 128), F32),
            dma((2,)),
            dma((4,)),
            dma((4,)),
            dma((4, 4)),
            dma((2, 8)),
            dma((2, 8)),
            dma((8,)),
            dma((8,)),
            dma((4, 5, 2)),
            dma((4, 5, 2)),
            dma((3, 3)),
            dma((3, 3)),
        ],
        compiler_params=pltpu.CompilerParams(
            collective_id=0, has_side_effects=True, vmem_limit_bytes=56 * 1024 * 1024
        ),
        cost_estimate=pl.CostEstimate(flops=4300000000, bytes_accessed=14000000, transcendentals=0),
    )(offset, interior, sources, absorption, bem_panel, incident, node_cell.reshape(32, 128))
    return pl.pallas_call(
        hand_over,
        out_shape=shapes,
        in_specs=[vmem] * 2,
        out_specs=(vmem,) * 2,
    )(*results)


def solution(mesh):
    in_specs = (
        P("slab", "blk", None),
        P("slab", "blk", None),
        P("slab", "blk", None),
        P("blk", "slab"),
        P("slab", None),
        P("slab"),
        P(),
    )
    out_specs = (P("slab", "blk", None), P(("blk", "slab"), None))
    return jax.shard_map(
        per_device, mesh=mesh, in_specs=in_specs, out_specs=out_specs, check_vma=False
    )
```

```python
import jax
import jax.numpy as jnp
from jax import lax
from jax.experimental import pallas as pl
from jax.experimental.pallas import tpu as pltpu
from jax.sharding import PartitionSpec as P

F32 = jnp.float32
BF16 = jnp.bfloat16
MESH = pl.DeviceIdType.MESH
CENTER = 8.0 / 3.0


def flip(pos, low, high):
    if low:
        pos = pos + 1 - 2 * lax.rem(pos, 2)
    if high:
        pos = 3 - pos
    return pos


XA, XB, YA, YB = ("x", 1, 0), ("x", 0, 1), ("y", 1, 0), ("y", 0, 1)
XAB, YAB = ("x", 1, 1), ("y", 1, 1)
ORDERS = ((XA, YA, XB, YB), (YA, XA, YB, XB), (XB, YB, XA, YA), (YB, XB, YA, XA))
NODES = 131072.0


def along_x(w, first, last):
    n = w.shape[1]
    left = jnp.where(first, 0.0, pltpu.roll(w, 1, 1))
    right = jnp.where(last, 0.0, pltpu.roll(w, n - 1, 1))
    return left + right


def kernel(
    offset, interior, sources, absorption, bem, incident, cells,
    relaxed_out, flux_out, relaxed, flux,
    pad1, pad2, src, inv, ytx1, ytx2, yrx1, yrx2,
    cell_v, ttx, trx, pieces, inc_v, panel,
    prod, rx1, rx2, rx3, rx4, rx5, mtx, mrx,
    out_sem, load_sem, inc_sem, panel_sem, halo_send, halo_recv,
    trace_send, trace_recv, rs_send, rs_recv, m_send, m_recv,
):
    slab, blk = lax.axis_index("slab"), lax.axis_index("blk")
    my_y, my_x, my_z = slab // 8, lax.rem(slab // 2, 4), lax.rem(slab, 2)

    def at(y, x, z):
        return y * 8 + x * 2 + z

    def toward(dim):
        if dim == "z":
            return (at(my_y, my_x, 1 - my_z), blk)
        axis, low, high = dim
        if axis == "x":
            return (at(my_y, flip(my_x, low, high), my_z), blk)
        return (at(flip(my_y, low, high), my_x, my_z), blk)

    up, down = lax.rem(slab + 1, 32), lax.rem(slab + 31, 32)
    east, west = lax.rem(blk + 1, 8), lax.rem(blk + 7, 8)

    core = pl.ds(8, 64)
    load_u = pltpu.make_async_copy(interior, pad1.at[pl.ds(1, 2), core], load_sem.at[0])
    load_c = pltpu.make_async_copy(cells, cell_v, load_sem.at[1])
    load_s = pltpu.make_async_copy(sources, src, load_sem.at[2])
    load_a = pltpu.make_async_copy(absorption, inv, load_sem.at[3])
    inc_load = pltpu.make_async_copy(incident, inc_v, inc_sem.at[0])
    panel_loads = {}
    order = sorted(((q, r) for q in range(4) for r in range(4)), key=lambda g: (-max(g), -g[0], -g[1]))
    for q, r in order:
        y = flip(my_y, q % 2, r % 2)
        x = flip(my_x, q // 2, r // 2)
        rows = pl.ds(pl.multiple_of(y * 256 + x * 64, 64), 64)
        panel_loads[q, r] = pltpu.make_async_copy(bem.at[rows], panel.at[q, r], panel_sem.at[q, r])
    load_u.start()
    load_c.start()
    inc_load.start()
    for group in order[:4]:
        panel_loads[group].start()

    partners = [(slab, lax.rem(blk + k, 8)) for k in range(1, 8)]
    partners += [toward(d) for d in (XA, XB, XAB, YA, YB, YAB, "z")]
    partners += [(up, blk), (down, blk), (up, east), (up, west), (down, east), (down, west)]
    barrier = pltpu.get_barrier_semaphore()
    for partner in partners:
        pl.semaphore_signal(barrier, inc=1, device_id=partner, device_id_type=MESH)

    load_u.wait()
    for z in range(2):
        for c in range(4):
            lanes = pl.ds(c * 128, 128)
            ytx1[0, pl.ds(z * 4 + c, 1), :] = pad1[1 + z, pl.ds(8, 1), lanes]
            ytx1[1, pl.ds(z * 4 + c, 1), :] = pad1[1 + z, pl.ds(71, 1), lanes]

    def halo_copies(sweep, pad, ytx, yrx):
        def copy(n, source, target, device):
            return pltpu.make_async_remote_copy(
                src_ref=source, dst_ref=target, send_sem=halo_send.at[sweep, n],
                recv_sem=halo_recv.at[sweep, n], device_id=device, device_id_type=MESH)
        return [
            copy(0, pad.at[2, core], pad.at[0, core], (up, blk)),
            copy(1, pad.at[1, core], pad.at[3, core], (down, blk)),
            copy(2, ytx.at[1], yrx.at[0], (slab, east)),
            copy(3, ytx.at[1], yrx.at[1], (up, east)),
            copy(4, ytx.at[1], yrx.at[2], (down, east)),
            copy(5, ytx.at[0], yrx.at[3], (slab, west)),
            copy(6, ytx.at[0], yrx.at[4], (up, west)),
            copy(7, ytx.at[0], yrx.at[5], (down, west)),
        ]

    halos1 = halo_copies(0, pad1, ytx1, yrx1)
    halos2 = halo_copies(1, pad2, ytx2, yrx2)
    pl.semaphore_wait(barrier, len(partners))
    def start_planes(halos, near):
        @pl.when(my_z == (0 if near else 1))
        def _():
            halos[0].start()

        @pl.when(my_z == (1 if near else 0))
        def _():
            halos[1].start()

    for copy in halos1[2:]:
        copy.start()
    start_planes(halos1, False)
    start_planes(halos1, True)

    for group in order[4:]:
        panel_loads[group].start()
    load_s.start()
    load_a.start()

    wanted = offset[0] // 4096 + blk // 4
    hit = jnp.full((8, 128), wanted, jnp.int32) == jnp.full((8, 128), slab, jnp.int32)
    coef = jnp.where(hit, 0.5, 0.0).astype(F32)[0:1, 0:1]
    jump_base = lax.rem(blk, 4) * 1024

    boxes = (rx1, rx2, rx3, rx4)
    chunks = (2, 2, 2, 1)
    waited = set()

    def arrived(part, stage, chunk):
        if chunk < chunks[stage] and (part, stage, chunk) not in waited:
            waited.add((part, stage, chunk))
            copies[part, stage, chunk].wait_recv()

    def rs_copy(part, stage, chunk):
        size = 512 >> stage
        piece = size // chunks[stage]
        start = size - (chunk + 1) * piece
        return pltpu.make_async_remote_copy(
            src_ref=prod.at[part, pl.ds(size + start, piece)],
            dst_ref=boxes[stage].at[part, pl.ds(start, piece)],
            send_sem=rs_send.at[part, stage, chunk], recv_sem=rs_recv.at[part, stage, chunk],
            device_id=toward(ORDERS[part][stage]), device_id_type=MESH)

    copies = {(p, s, c): rs_copy(p, s, c) for p in range(4) for s in range(4) for c in range(chunks[s])}

    def swapped(q):
        return (q % 2) * 2 + q // 2

    def unit(pair, q):
        for r in range(4):
            copy = panel_loads.pop((q, r) if pair == 0 else (r, q), None)
            if copy is not None:
                copy.wait()
        lhs = panel[q] if pair == 0 else panel[:, q]
        cols = pl.ds(pair * 256, 256)
        out = jnp.dot(lhs.reshape(256, 4096), inc_v[:, cols], preferred_element_type=F32)
        for r in range(4):
            qa, qb = (q, r) if pair == 0 else (r, q)
            y = flip(my_y, qa % 2, qb % 2)
            x = flip(my_x, qa // 2, qb // 2)
            rows = pl.ds(pl.multiple_of(jump_base + y * 256 + x * 64, 64), 64)
            piece = out[r * 64:(r + 1) * 64] + coef * inc_v[rows, cols].astype(F32)
            prod[pair * 2, pl.ds(q * 256 + r * 64, 64), :] = piece[:, :128]
            prod[pair * 2 + 1, pl.ds(swapped(q) * 256 + swapped(r) * 64, 64), :] = piece[:, 128:]

    def first_units(pair):
        unit(pair, 3)
        copies[pair * 2, 0, 0].start()
        copies[pair * 2 + 1, 0, 0].start()

    load_c.wait()
    y_index = lax.broadcasted_iota(jnp.int32, (64, 128), 0) * 2
    totals = [jnp.zeros((64, 128), F32)] * 4
    for z in range(2):
        for side in range(2):
            face = jnp.broadcast_to(pad1[1 + z, pl.ds(8, 64), pl.ds(511 * side, 1)], (64, 128))
            for c in range(4):
                cell = cell_v[pl.ds(blk * 4 + c, 1), :]
                totals[c] += jnp.where(cell == y_index + (z * 128 + side), face, 0.0)
    found = [jnp.sum(total, axis=0, keepdims=True) for total in totals]
    for c in range(4):
        ttx[pl.ds(c, 1), :] = found[c]

    inc_load.wait()
    turned = jnp.concatenate(found + [jnp.zeros((124, 128), F32)], axis=0).T
    squares = jnp.zeros((8, 512), F32)
    for c in range(4):
        rows = pl.ds(pl.multiple_of(blk * 512 + c * 128, 128), 128)
        column = lax.slice(turned, (0, c), (128, c + 1))
        x = (inc_v[rows, :].astype(F32) + column).astype(BF16).astype(F32)
        squares += jnp.sum((x * x).reshape(16, 8, 512), axis=0)
    squares = jnp.sum(squares, axis=0, keepdims=True)
    for c in range(4):
        ttx[pl.ds(4 + c, 1), :] = squares[:, c * 128:(c + 1) * 128]
    trx[0] = ttx[...]

    traces = []
    for k in range(1, 8):
        traces.append(pltpu.make_async_remote_copy(
            src_ref=ttx, dst_ref=trx.at[k], send_sem=trace_send.at[k], recv_sem=trace_recv.at[k],
            device_id=(slab, lax.rem(blk + k, 8)), device_id_type=MESH))
        traces[-1].start()

    for pair in range(2):
        first_units(pair)
    for pair in range(2):
        unit(pair, 2)
        copies[pair * 2, 0, 1].start()
    for pair in range(2):
        unit(pair, 1)
        copies[pair * 2 + 1, 0, 1].start()
    for pair in range(2):
        unit(pair, 0)

    lane = lax.broadcasted_iota(jnp.int32, (64, 512), 1)
    first, last = lane == 0, lane == 511
    keep_down = jnp.where(slab > 0, 1.0, 0.0).astype(F32)
    keep_up = jnp.where(slab < 31, 1.0, 0.0).astype(F32)
    keep_west = jnp.where(blk > 0, 1.0, 0.0).astype(F32)
    keep_east = jnp.where(blk < 7, 1.0, 0.0).astype(F32)

    def sweep(pad, yrx, halos, store):
        for copy in halos:
            copy.wait_recv()
        for c in range(4):
            lanes = pl.ds(c * 128, 128)
            for row, base, keep in ((7, 0, keep_west), (72, 3, keep_east)):
                one = pl.ds(row, 1)
                pad[0, one, lanes] = yrx[base + 1, pl.ds(4 + c, 1), :] * keep
                pad[1, one, lanes] = yrx[base, pl.ds(c, 1), :] * keep
                pad[2, one, lanes] = yrx[base, pl.ds(4 + c, 1), :] * keep
                pad[3, one, lanes] = yrx[base + 2, pl.ds(c, 1), :] * keep

        def beside(z):
            v = pad[z, pl.ds(8, 64), :]
            s = pad[z, pl.ds(7, 64), :] + pad[z, pl.ds(9, 64), :]
            across = s * (1.0 / 6.0) + along_x(v * (1.0 / 6.0) + s * (1.0 / 12.0), first, last)
            return v, s, across

        low = beside(0)[2] * keep_down
        v0, s0, q0 = beside(1)
        v1, s1, q1 = beside(2)
        high = beside(3)[2] * keep_up
        e0 = low + q1 + along_x(s0, first, last) * (1.0 / 6.0)
        e1 = q0 + high + along_x(s1, first, last) * (1.0 / 6.0)
        store(0, 0.4 * v0 + inv[0] * (src[0] + e0))
        store(1, 0.4 * v1 + inv[1] * (src[1] + e1))

    def sweep_first():
        load_s.wait()
        load_a.wait()
        inv[...] = 0.6 / (CENTER + inv[...])

        def store(z, value):
            pad2[1 + z, pl.ds(8, 64), :] = value

        sweep(pad1, yrx1, halos1, store)
        for z in range(2):
            for c in range(4):
                lanes = pl.ds(c * 128, 128)
                ytx2[0, pl.ds(z * 4 + c, 1), :] = pad2[1 + z, pl.ds(8, 1), lanes]
                ytx2[1, pl.ds(z * 4 + c, 1), :] = pad2[1 + z, pl.ds(71, 1), lanes]
        for copy in halos2[2:]:
            copy.start()
        start_planes(halos2, False)
        start_planes(halos2, True)

    relaxed_copy = pltpu.make_async_copy(relaxed, relaxed_out, out_sem.at[0])
    flux_copy = pltpu.make_async_copy(flux, flux_out, out_sem.at[1])

    def sweep_second():
        def store(z, value):
            relaxed[z] = value

        sweep(pad2, yrx2, halos2, store)
        relaxed_copy.start()

    groups = ([XA, XB, XAB], [YA, YB, YAB], ["z"])
    sends = [
        [
            pltpu.make_async_remote_copy(
                src_ref=mtx.at[s], dst_ref=mrx.at[s, n], send_sem=m_send.at[s, n], recv_sem=m_recv.at[s, n],
                device_id=toward(d), device_id_type=MESH)
            for n, d in enumerate(group)
        ]
        for s, group in enumerate(groups)
    ]

    def trace_products():
        for copy in traces:
            copy.wait_recv()
        pieces[...] = jnp.zeros((16, 4096), F32)
        squares = trx[0, pl.ds(4, 4), :]
        for k in range(1, 8):
            squares += trx[k, pl.ds(4, 4), :]
        for k in range(8):
            base = lax.rem(blk + 8 - k, 8) * 512
            for c in range(4):
                lanes = pl.ds(pl.multiple_of(base + c * 128, 128), 128)
                rest = trx[k, pl.ds(c, 1), :]
                for n in range(3):
                    piece = rest.astype(BF16).astype(F32)
                    pieces[pl.ds(n, 1), lanes] = piece
                    rest = rest - piece
        spread = lax.dot_general(
            pieces[...].astype(BF16), panel[...].reshape(1024, 4096), (((1,), (1,)), ((), ())),
            preferred_element_type=F32)
        row = spread[0:1] + spread[1:2] + spread[2:3]
        mtx[0] = jnp.zeros((24, 128), F32)
        mtx[0, pl.ds(0, 4), :] = squares
        for q in range(4):
            for r in range(4):
                y = flip(my_y, q % 2, r % 2)
                x = flip(my_x, q // 2, r // 2)
                g = q * 4 + r
                mtx[0, pl.ds(8 + y * 4 + x, 1), pl.ds(0, 64)] = row[:, g * 64:(g + 1) * 64]
        for g in range(16):
            k = lax.rem(blk + 8 - (lax.rem(blk, 4) * 2 + g // 8), 8)
            there = trx[k, pl.ds(g % 8 // 2, 1), :][:, g % 2 * 64:g % 2 * 64 + 64]
            mtx[0, pl.ds(8 + g, 1), pl.ds(0, 64)] += coef * there
        for copy in sends[0]:
            copy.start()

    def message_sum(s):
        total = mtx[s]
        for n, copy in enumerate(sends[s]):
            copy.wait_recv()
            total += mrx[s, n]
        return total

    def message_step(s):
        mtx[s] = message_sum(s - 1)
        for copy in sends[s]:
            copy.start()

    def added(part, rows, stages):
        total = prod[part, rows, :]
        for stage in range(stages):
            total += boxes[stage][part, rows, :]
        return total

    def halving(stage):
        size = 512 >> stage
        for part in range(4):
            if stage >= 2:
                arrived(part, stage - 2, 1)
            arrived(part, stage - 1, 0)
            piece = size // chunks[stage]
            for chunk in range(chunks[stage]):
                rows = pl.ds(2 * size - (chunk + 1) * piece, piece)
                prod[part, rows, :] = added(part, rows, stage)
                copies[part, stage, chunk].start()

    own = pl.ds(pl.multiple_of(my_z * 32, 32), 32)
    other = pl.ds(pl.multiple_of((1 - my_z) * 32, 32), 32)
    z_copies = [
        pltpu.make_async_remote_copy(
            src_ref=prod.at[part, other], dst_ref=rx5.at[part],
            send_sem=rs_send.at[part, 4, 0], recv_sem=rs_recv.at[part, 4, 0],
            device_id=toward("z"), device_id_type=MESH)
        for part in range(4)
    ]

    def last_halving():
        for part in range(4):
            arrived(part, 2, 1)
            arrived(part, 3, 0)
            arrived(part, 3, 1)
            prod[part, other, :] = added(part, other, 4)
            z_copies[part].start()

    def finish():
        message = message_sum(2)
        mtx[3] = message
        row = mtx[3, pl.ds(8 + my_y * 4 + my_x, 1), :]
        here = lax.broadcasted_iota(jnp.int32, (32, 128), 1) == (
            lax.broadcasted_iota(jnp.int32, (32, 128), 0) + 32 * my_z)
        column = jnp.sum(jnp.where(here, row, 0.0), axis=1, keepdims=True)
        for part in range(4):
            scale = 1.0 / jnp.sqrt(message[part:part + 1] / NODES + 1e-06)
            z_copies[part].wait_recv()
            flux[:, pl.ds(part * 128, 128)] = (added(part, own, 4) + rx5[part] + column) * scale
        flux_copy.start()

    def sent(group):
        for copy in group:
            copy.wait_send()

    def stage_copies(stage):
        return [copies[p, stage, c] for p in range(4) for c in range(chunks[stage])]

    halving(1)
    trace_products()
    sweep_first()
    halving(2)
    sent(traces + halos1 + stage_copies(0))
    message_step(1)
    halving(3)
    sent(sends[0] + stage_copies(1))
    last_halving()
    message_step(2)
    sent(sends[1] + halos2 + stage_copies(2))
    sweep_second()
    finish()

    sent(sends[2] + stage_copies(3) + z_copies)
    relaxed_copy.wait()
    flux_copy.wait()


def hand_over(relaxed, flux, relaxed_out, flux_out):
    relaxed_out[...] = relaxed[...]
    flux_out[...] = flux[...]


def per_device(interior, sources, absorption, bem_panel, incident, node_cell, offset):
    any_space = pl.BlockSpec(memory_space=pl.ANY)
    vmem = pl.BlockSpec(memory_space=pltpu.VMEM)
    dma = pltpu.SemaphoreType.DMA
    shapes = (
        jax.ShapeDtypeStruct((2, 64, 512), F32),
        jax.ShapeDtypeStruct((32, 512), F32),
    )
    results = pl.pallas_call(
        kernel,
        out_shape=shapes,
        in_specs=[pl.BlockSpec(memory_space=pltpu.SMEM)] + [any_space] * 6,
        out_specs=(any_space, any_space),
        scratch_shapes=[
            pltpu.VMEM((2, 64, 512), F32),
            pltpu.VMEM((32, 512), F32),
            pltpu.VMEM((4, 80, 512), F32),
            pltpu.VMEM((4, 80, 512), F32),
            pltpu.VMEM((2, 64, 512), F32),
            pltpu.VMEM((2, 64, 512), F32),
            pltpu.VMEM((2, 8, 128), F32),
            pltpu.VMEM((2, 8, 128), F32),
            pltpu.VMEM((6, 8, 128), F32),
            pltpu.VMEM((6, 8, 128), F32),
            pltpu.VMEM((32, 128), jnp.int32),
            pltpu.VMEM((8, 128), F32),
            pltpu.VMEM((8, 8, 128), F32),
            pltpu.VMEM((16, 4096), F32),
            pltpu.VMEM((4096, 512), BF16),
            pltpu.VMEM((4, 4, 64, 4096), BF16),
            pltpu.VMEM((4, 1024, 128), F32),
            pltpu.VMEM((4, 512, 128), F32),
            pltpu.VMEM((4, 256, 128), F32),
            pltpu.VMEM((4, 128, 128), F32),
            pltpu.VMEM((4, 64, 128), F32),
            pltpu.VMEM((4, 32, 128), F32),
            pltpu.VMEM((4, 24, 128), F32),
            pltpu.VMEM((3, 3, 24, 128), F32),
            dma((2,)),
            dma((4,)),
            dma((4,)),
            dma((4, 4)),
            dma((2, 8)),
            dma((2, 8)),
            dma((8,)),
            dma((8,)),
            dma((4, 5, 2)),
            dma((4, 5, 2)),
            dma((3, 3)),
            dma((3, 3)),
        ],
        compiler_params=pltpu.CompilerParams(
            collective_id=0, has_side_effects=True, vmem_limit_bytes=56 * 1024 * 1024
        ),
        cost_estimate=pl.CostEstimate(flops=4300000000, bytes_accessed=14000000, transcendentals=0),
    )(offset, interior, sources, absorption, bem_panel, incident, node_cell.reshape(32, 128))
    return pl.pallas_call(
        hand_over,
        out_shape=shapes,
        in_specs=[vmem] * 2,
        out_specs=(vmem,) * 2,
    )(*results)


def solution(mesh):
    in_specs = (
        P("slab", "blk", None),
        P("slab", "blk", None),
        P("slab", "blk", None),
        P("blk", "slab"),
        P("slab", None),
        P("slab"),
        P(),
    )
    out_specs = (P("slab", "blk", None), P(("blk", "slab"), None))
    return jax.shard_map(
        per_device, mesh=mesh, in_specs=in_specs, out_specs=out_specs, check_vma=False
    )
```
